32 devices in a mesh: groups: 1, rows: 32 (over z, y, x, core).
Axes of the slice: x: 2, y: 2, z: 4, core: 2. Of those that a mesh axis runs over, the one named last changes fastest.
Arguments:
- prompt: bfloat16 [16, 8192], P('groups'), may hold values from -6 to 6
- gate_weight: bfloat16 [8192, 4096], P(None, 'rows'), may hold values from -0.0625 to 0.0625
- up_weight: bfloat16 [8192, 4096], P(None, 'rows'), may hold values from -0.0625 to 0.0625
- down_weight: bfloat16 [4096, 8192], P('rows'), may hold values from -0.09375 to 0.09375
- proj_blocks: bfloat16 [3072, 128, 128], P('rows'), may hold values from -0.29882812 to 0.29882812
- proj_column: int32 [3072, 1], P('rows'), may hold values from 0 to 31; in each aligned block of 96 rows (0 to 95, 96 to 191, ...) at most 3 rows name the same one
- proj_row: int32 [3072], P('rows'), may hold values from 0 to 63
- proj_variant: int32 [3072], P('rows'), may hold values from 0 to 22
- proj_kind: int32 [3072], P('rows'), may hold values from 0 to 1
- down_blocks: bfloat16 [3072, 128, 128], P('rows'), may hold values from -0.59765625 to 0.59765625
- down_row: int32 [3072, 1], P('rows'), may hold values from 0 to 31; in each aligned block of 96 rows (0 to 95, 96 to 191, ...) at most 3 rows name the same one
- down_column: int32 [3072], P('rows'), may hold values from 0 to 63
- down_variant: int32 [3072], P('rows'), may hold values from 0 to 22
Outputs:
- screened: bfloat16 [384, 8192], P(('groups', 'rows'))
The draws below stay inside these ranges and needn't reach their ends.
Inputs may be any that keep to these rules, and one draw needn't show every extreme that they name: `proj_column`: among the 96 gate and up blocks stored by one device, no hidden block is named more than 3 times, and in every draw some device names some hidden block exactly 3 times. `down_row`: among the 96 down blocks stored by one device, no hidden block is named more than 3 times, and in every draw some device names some hidden block exactly 3 times.
All inputs are finite; a program needn't handle non-finite values.
Results may differ from the reference program's by a relative error of at most 0.0051.
Values may be sent and summed in bfloat16 or wider, within the bound.
A program may use at most 128 MiB of HBM per device.

```python
import math
import jax
import jax.numpy as jnp
import numpy as np
from jax import lax

D = 8192
BLK = 128
FF = 4096
DB = 64
P_SIZE = 16
VARIANTS = 23
SETS = 24
S1 = 96
S2 = 96
CAP1 = 3
CAP2 = 3
TOTAL1 = 3072
TOTAL2 = 3072


def touch_ends(result, own_key, smallest, high):
    longest = result.shape.index(max(result.shape))
    spots = []
    for shift in (0, 1):
        where = [jax.random.randint(jax.random.fold_in(own_key, axis), (), 0, length) for axis, length in enumerate(result.shape)]
        where[longest] = (where[longest] + shift) % result.shape[longest]
        spots.append(tuple(where))
    return result.at[spots[0]].set(smallest).at[spots[1]].set(high)


def shard_levels(stream_key, shape, shards, low, largest):
    factor_of, own = 1.0, jax.random.fold_in(stream_key, 6)
    for dim, parts in shards:
        steps = jnp.exp(jax.random.uniform(jax.random.fold_in(own, dim), (parts,), jnp.float32, low / len(shards), largest / len(shards)))
        factor_of = factor_of * jnp.repeat(steps, shape[dim] // parts).reshape([-1 if axis == dim else 1 for axis in range(len(shape))])
    return factor_of


def assign_block(own_key, own, number, rows, count, top, limit, skew):
    ranking = jax.random.permutation(own_key, count)
    packed, usual = load_shares(count, rows * top, limit, skew, True), load_shares(count, rows * top, limit, skew, False)
    places = jnp.arange(count)

    def named(tallies, rotation):
        used = int((tallies > 0).sum())
        fixed = max(1, used // 4)
        passed = fixed + (places - fixed + rotation * (used - fixed)) % max(1, count - fixed)
        return jnp.zeros((count,), jnp.int32).at[ranking[jnp.where(places < fixed, places, passed)]].set(jnp.asarray(tallies, jnp.int32))

    tallies = jnp.where(number % 4 == 0, named(packed, number // 4), named(usual, number - number // 4 - 1))
    mixed = jax.random.permutation(jax.random.fold_in(own, 3), count)
    source_of, receiver = mixed[0:count // 2 * 2:2], mixed[1:count // 2 * 2:2]
    margin = jnp.minimum(tallies[source_of] - 1, limit - tallies[receiver]) // 2
    margin = jnp.where((source_of == ranking[0]) | (receiver == ranking[0]) | (tallies[receiver] == 0), 0, jnp.maximum(margin, 0))
    passed = jax.random.randint(jax.random.fold_in(own, 4), (count // 2,), 0, 1 << 20) % (margin + 1)
    tallies = tallies.at[source_of].add(-passed).at[receiver].add(passed)
    members = jnp.searchsorted(jnp.cumsum(tallies), jnp.arange(rows * top), side="right").astype(jnp.int32)
    listing = members.reshape(top, rows).T
    listing = listing[jax.random.permutation(jax.random.fold_in(own, 1), rows)]
    rotation = jax.random.randint(jax.random.fold_in(own, 2), (rows, 1), 0, top)
    return jnp.take_along_axis(listing, (jnp.arange(top)[None, :] + rotation) % top, axis=1)


def load_shares(amount, total, limit, lean, full):
    weights = [(1 << 20) // math.isqrt(grade ** lean) + 1 for grade in range(1, amount + 1)]
    largest = limit if full else min(limit, max(-(-total // amount), total * weights[0] // sum(weights)))
    least = 1 if total - largest >= amount - 1 else 0
    holding, spare = [largest] + [least] * (amount - 1), total - largest - least * (amount - 1)
    while spare > 0:
        movable = [i for i in range(1, amount) if holding[i] < largest] or [i for i in range(1, amount) if holding[i] < limit]
        pool, remaining = sum([weights[i] for i in movable]), spare
        for i in movable:
            more = min(limit - holding[i], max(1, remaining * weights[i] // pool), spare)
            holding[i] = holding[i] + more
            spare = spare - more
    return np.array(holding)


def bell_draw(stream_key, dims, spread, bound, cuts=(), kind=jnp.bfloat16):
    gain = shard_levels(stream_key, dims, cuts, -0.22, 0.18) if cuts else 1.0
    entries = jax.random.normal(stream_key, dims, jnp.float32) * spread * gain
    return jnp.minimum(jnp.maximum(entries, -bound), bound).astype(kind)


def setup_inputs(seed: int = 0, part: int = 0) -> dict:
    arg_keys = jax.random.split(jax.random.key(seed), 14)
    part_keys = jax.random.split(jax.random.fold_in(arg_keys[13], part), 14)
    prompt = bell_draw(part_keys[0], (P_SIZE, D), 1.0, 6.0)
    gate_weight = bell_draw(arg_keys[1], (D, FF), D ** -0.5, 0.0625, ((1, 32),))
    up_weight = bell_draw(arg_keys[2], (D, FF), D ** -0.5, 0.0625, ((1, 32),))
    down_weight = bell_draw(arg_keys[3], (FF, D), FF ** -0.5, 0.09375, ((0, 32),))
    proj_blocks = bell_draw(arg_keys[4], (TOTAL1, BLK, BLK), 0.05, 0.29882812, ((0, 32),))
    proj_column_keys = jax.random.split(jax.random.fold_in(arg_keys[5], 1), TOTAL1 // S1)
    proj_column_turns = jax.random.permutation(jax.random.fold_in(arg_keys[5], 3), TOTAL1 // S1)
    proj_column = jax.vmap(lambda own, number: assign_block(jax.random.fold_in(arg_keys[5], 2), own, number, S1, FF // BLK, 1, CAP1, 2))(proj_column_keys, proj_column_turns).reshape((TOTAL1, 1))
    proj_row = touch_ends(jax.random.randint(arg_keys[6], (TOTAL1,), 0, DB), jax.random.fold_in(arg_keys[6], 1), 0, DB - 1).astype(jnp.int32)
    proj_variant = touch_ends(jax.random.randint(arg_keys[7], (TOTAL1,), 0, VARIANTS), jax.random.fold_in(arg_keys[7], 1), 0, VARIANTS - 1).astype(jnp.int32)
    proj_kind = touch_ends(jax.random.randint(arg_keys[8], (TOTAL1,), 0, 2), jax.random.fold_in(arg_keys[8], 1), 0, 1).astype(jnp.int32)
    down_blocks = bell_draw(arg_keys[9], (TOTAL2, BLK, BLK), 0.1, 0.59765625, ((0, 32),))
    down_row_keys = jax.random.split(jax.random.fold_in(arg_keys[10], 1), TOTAL2 // S2)
    down_row_turns = jax.random.permutation(jax.random.fold_in(arg_keys[10], 3), TOTAL2 // S2)
    down_row = jax.vmap(lambda own, number: assign_block(jax.random.fold_in(arg_keys[10], 2), own, number, S2, FF // BLK, 1, CAP2, 2))(down_row_keys, down_row_turns).reshape((TOTAL2, 1))
    down_column = touch_ends(jax.random.randint(arg_keys[11], (TOTAL2,), 0, DB), jax.random.fold_in(arg_keys[11], 1), 0, DB - 1).astype(jnp.int32)
    down_variant = touch_ends(jax.random.randint(arg_keys[12], (TOTAL2,), 0, VARIANTS), jax.random.fold_in(arg_keys[12], 1), 0, VARIANTS - 1).astype(jnp.int32)
    return {"prompt": prompt, "gate_weight": gate_weight, "up_weight": up_weight, "down_weight": down_weight, "proj_blocks": proj_blocks, "proj_column": proj_column, "proj_row": proj_row, "proj_variant": proj_variant, "proj_kind": proj_kind, "down_blocks": down_blocks, "down_row": down_row, "down_column": down_column, "down_variant": down_variant}


def reference(prompt, gate_weight, up_weight, down_weight, proj_blocks, proj_column, proj_row, proj_variant, proj_kind, down_blocks, down_row, down_column, down_variant):
    block_count = FF // BLK
    gate_base = jnp.dot(prompt, gate_weight, preferred_element_type=jnp.float32)
    up_base = jnp.dot(prompt, up_weight, preferred_element_type=jnp.float32)
    prompt_blocks = prompt.reshape(P_SIZE, DB, BLK).astype(jnp.float32)
    chosen = jnp.take(prompt_blocks, proj_row.astype(jnp.int32), axis=1)
    products = jnp.einsum("psd,sdf->spf", chosen, proj_blocks.astype(jnp.float32), precision=lax.Precision.HIGHEST)
    extra = jnp.zeros((2, VARIANTS, P_SIZE, block_count, BLK), jnp.float32)
    extra = extra.at[proj_kind.astype(jnp.int32), proj_variant.astype(jnp.int32), :, proj_column[:, 0].astype(jnp.int32)].add(products)
    zero_set = jnp.zeros((1, P_SIZE, FF), jnp.float32)
    gate_values = gate_base[None] + jnp.concatenate([zero_set, extra[0].reshape(VARIANTS, P_SIZE, FF)], axis=0)
    up_values = up_base[None] + jnp.concatenate([zero_set, extra[1].reshape(VARIANTS, P_SIZE, FF)], axis=0)
    hidden = (jax.nn.silu(gate_values) * up_values).astype(jnp.bfloat16)
    dense = jnp.dot(hidden.reshape(SETS * P_SIZE, FF), down_weight, preferred_element_type=jnp.float32)
    hidden_blocks = hidden.reshape(SETS, P_SIZE, block_count, BLK)
    chosen_hidden = hidden_blocks[down_variant.astype(jnp.int32) + 1, :, down_row[:, 0].astype(jnp.int32)]
    corrections = jnp.einsum("spf,sfd->spd", chosen_hidden.astype(jnp.float32), down_blocks.astype(jnp.float32), precision=lax.Precision.HIGHEST)
    down_extra = jnp.zeros((SETS, P_SIZE, DB, BLK), jnp.float32)
    down_extra = down_extra.at[down_variant.astype(jnp.int32) + 1, :, down_column.astype(jnp.int32)].add(corrections)
    return (dense + down_extra.reshape(SETS * P_SIZE, D)).astype(jnp.bfloat16)
```

```python
import functools

import jax
import jax.numpy as jnp
from jax import lax
from jax.experimental import pallas as pl
from jax.experimental.pallas import tpu as pltpu
from jax.sharding import PartitionSpec as P

VARIANTS = 23
UNIT_ROWS = 48
LANES = 4
VMEM_LIMIT = 56 * 1024 * 1024


def slot_places(targets, capacity):
    order = jnp.arange(targets.shape[0])
    earlier = (targets[:, None] == targets[None, :]) & (order[None, :] < order[:, None])
    return targets * capacity + jnp.sum(earlier.astype(jnp.int32), axis=1)


def down_kernel(device_count, row_ref, column_ref, variant_ref, all_ref, own_ref, weight_ref, block_ref, out_ref, acc):
    total_rows, model_width = acc.shape
    tile = 1024

    def dense(step, _):
        columns = pl.ds(pl.multiple_of(step * tile, tile), tile)
        acc[:, columns] = jnp.dot(own_ref[...], weight_ref[:, columns], preferred_element_type=jnp.float32)
        return 0

    lax.fori_loop(0, model_width // tile, dense, 0)
    slots = block_ref.shape[0]
    batch = 8

    def correct(step, _):
        parts = []
        for i in range(batch):
            j = step * batch + i
            first = pl.multiple_of((variant_ref[j] + 1) * 16, 16)
            rows = all_ref[row_ref[j], pl.ds(first, 16), :]
            parts.append((j, first, jnp.dot(rows, block_ref[j], preferred_element_type=jnp.float32)))
        for j, first, part in parts:
            columns = pl.ds(pl.multiple_of(column_ref[j] * 128, 128), 128)
            acc[pl.ds(first, 16), columns] += part
        return 0

    lax.fori_loop(0, slots // batch, correct, 0)
    own_rows = total_rows // device_count
    pieces = UNIT_ROWS // own_rows
    width = model_width // pieces
    narrow = width // LANES
    owners = 24 // own_rows

    def pack(step, _):
        first = pl.multiple_of(step * 24, 24)
        for owner in range(owners):
            place = step * (owners // 2) + owner // 2
            for channel in range(LANES):
                low = channel * narrow
                parts = [
                    acc[pl.ds(first, 24), piece * width + low : piece * width + low + narrow][
                        owner * own_rows : (owner + 1) * own_rows
                    ]
                    for piece in range(pieces)
                ]
                out_ref[channel, owner % 2, place] = jnp.concatenate(parts, axis=0).astype(jnp.bfloat16)
        return 0

    lax.fori_loop(0, total_rows // 24, pack, 0)


def down_partial(device_count, row, column, variant, gathered, own, weight, blocks):
    total_rows = own.shape[0]
    model_width = weight.shape[1]
    width = model_width * (total_rows // device_count) // UNIT_ROWS
    return pl.pallas_call(
        functools.partial(down_kernel, device_count),
        out_shape=jax.ShapeDtypeStruct(
            (LANES, 2, device_count // 2, UNIT_ROWS, width // LANES), jnp.bfloat16
        ),
        in_specs=[pl.BlockSpec(memory_space=pltpu.SMEM)] * 3 + [pl.BlockSpec(memory_space=pltpu.VMEM)] * 4,
        out_specs=pl.BlockSpec(memory_space=pltpu.VMEM),
        scratch_shapes=[pltpu.VMEM((total_rows, model_width), jnp.float32)],
        compiler_params=pltpu.CompilerParams(vmem_limit_bytes=VMEM_LIMIT),
    )(row, column, variant, gathered, own, weight, blocks)


def bit_orders(device_count):
    if device_count == 32:
        return [[0, 1, 2, 3, 4], [0, 2, 1, 3, 4]]
    bits = device_count.bit_length() - 1
    middle = (bits + 1) // 2
    first, second = list(range(1, middle)), list(range(middle, bits))
    return [[0] + first + second, [0] + second + first]


def scatter_kernel(device_count, part_ref, out_ref, *scratch):
    stages = device_count.bit_length() - 1
    received = scratch[:stages]
    sending = (None,) + scratch[stages : 2 * stages - 1]
    kept = (None,) + scratch[2 * stages - 1 : 3 * stages - 2]
    send_sem, recv_sem = scratch[3 * stages - 2 :]
    me = lax.axis_index("rows")
    half = device_count // 2
    orders = [bit_orders(device_count)[c % 2] for c in range(LANES)]
    my_bits = [(me // (1 << b)) % 2 for b in range(stages)]
    partners = [me + (1 - 2 * my_bits[b]) * (1 << b) for b in range(stages)]

    barrier = pltpu.get_barrier_semaphore()
    for b in range(stages):
        pl.semaphore_signal(barrier, inc=1, device_id={"rows": partners[b]}, device_id_type=pl.DeviceIdType.MESH)
    pl.semaphore_wait(barrier, stages)

    def transfer(channel, stage):
        source = part_ref.at[channel, 1 - my_bits[0]] if stage == 0 else sending[stage].at[channel]
        return pltpu.make_async_remote_copy(
            src_ref=source,
            dst_ref=received[stage].at[channel],
            send_sem=send_sem.at[channel, stage],
            recv_sem=recv_sem.at[channel, stage],
            device_id={"rows": partners[orders[channel][stage]]},
            device_id_type=pl.DeviceIdType.MESH,
        )

    copies = {}
    for channel in range(LANES):
        copies[channel, 0] = transfer(channel, 0)
        copies[channel, 0].start()
    for stage in range(stages):
        count = half >> stage
        for channel in range(LANES):
            copies[channel, stage].wait_recv()

            def value(i):
                if stage == 0:
                    mine = part_ref[channel, my_bits[0], i].astype(jnp.float32)
                else:
                    mine = kept[stage][channel, i]
                return mine + received[stage][channel, i].astype(jnp.float32)

            if stage == stages - 1:
                out_ref[channel] = value(0).astype(jnp.bfloat16)
                continue
            bit = orders[channel][stage + 1]
            low = 1 << sum(1 for other in orders[channel][stage + 2 :] if other < bit)

            def pick(j, side):
                return (j // low) * (2 * low) + side * low + j % low

            def send_side(j, _):
                sending[stage + 1][channel, j] = value(pick(j, 1 - my_bits[bit])).astype(jnp.bfloat16)
                return 0

            def keep_side(j, _):
                kept[stage + 1][channel, j] = value(pick(j, my_bits[bit]))
                return 0

            lax.fori_loop(0, count // 2, send_side, 0)
            copies[channel, stage + 1] = transfer(channel, stage + 1)
            copies[channel, stage + 1].start()
            lax.fori_loop(0, count // 2, keep_side, 0)
    for copy in copies.values():
        copy.wait_send()


def reduce_scatter(device_count, part):
    narrow = part.shape[-1]
    stages = device_count.bit_length() - 1
    half = device_count // 2
    counts = [half >> s for s in range(stages)]
    scratch = [pltpu.VMEM((LANES, k, UNIT_ROWS, narrow), jnp.bfloat16) for k in counts]
    scratch += [pltpu.VMEM((LANES, k, UNIT_ROWS, narrow), jnp.bfloat16) for k in counts[1:]]
    scratch += [pltpu.VMEM((LANES, k, UNIT_ROWS, narrow), jnp.float32) for k in counts[1:]]
    scratch += [pltpu.SemaphoreType.DMA((LANES, stages))] * 2
    return pl.pallas_call(
        functools.partial(scatter_kernel, device_count),
        out_shape=jax.ShapeDtypeStruct((LANES, UNIT_ROWS, narrow), jnp.bfloat16),
        in_specs=[pl.BlockSpec(memory_space=pltpu.VMEM)],
        out_specs=pl.BlockSpec(memory_space=pltpu.VMEM),
        scratch_shapes=scratch,
        compiler_params=pltpu.CompilerParams(
            collective_id=0, has_side_effects=True, vmem_limit_bytes=VMEM_LIMIT
        ),
    )(part)


def on_device(
    prompt,
    gate_weight,
    up_weight,
    down_weight,
    proj_blocks,
    proj_column,
    proj_row,
    proj_variant,
    proj_kind,
    down_blocks,
    down_row,
    down_column,
    down_variant,
):
    device_count = lax.axis_size("rows")
    block_size = proj_blocks.shape[1]
    tokens, model_width = prompt.shape
    width_blocks = model_width // block_size
    set_count = VARIANTS + 1
    slots = proj_blocks.shape[0]
    capacity = max(2, -(-slots // device_count))
    places = device_count * capacity

    prompt_blocks = prompt.reshape(tokens, width_blocks, block_size).transpose(1, 0, 2)
    chosen = jnp.take(prompt_blocks, proj_row, axis=0)
    products = jnp.einsum("spd,sdf->spf", chosen, proj_blocks, preferred_element_type=jnp.float32)
    codes = (proj_variant * 2 + proj_kind + 2).astype(jnp.bfloat16)
    payload = jnp.concatenate(
        [
            products.astype(jnp.bfloat16).reshape(slots, tokens * block_size),
            jnp.broadcast_to(codes[:, None], (slots, block_size)),
        ],
        axis=1,
    )
    place_of = slot_places(proj_column[:, 0], capacity)
    spread = (jnp.arange(places)[:, None] == place_of[None, :]).astype(jnp.bfloat16)
    sent = jnp.dot(spread, payload, preferred_element_type=jnp.float32).astype(jnp.bfloat16)
    got = lax.all_to_all(sent, "rows", split_axis=0, concat_axis=0, tiled=True)
    got_codes = got[:, tokens * block_size].astype(jnp.int32)
    values = got[:, : tokens * block_size]
    pick = (got_codes[None, :] == jnp.arange(2 * set_count)[:, None]).astype(jnp.bfloat16)
    pick = pick * (jnp.arange(2 * set_count)[:, None] >= 2).astype(jnp.bfloat16)
    extra = jnp.dot(pick, values, preferred_element_type=jnp.float32)
    extra = extra.reshape(set_count, 2, tokens, block_size)
    gate_base = jnp.dot(prompt, gate_weight, preferred_element_type=jnp.float32)
    up_base = jnp.dot(prompt, up_weight, preferred_element_type=jnp.float32)
    gate_values = gate_base[None] + extra[:, 0]
    up_values = up_base[None] + extra[:, 1]
    hidden = (jax.nn.silu(gate_values) * up_values).astype(jnp.bfloat16)
    hidden = hidden.reshape(set_count * tokens, block_size)
    gathered = lax.all_gather(hidden, "rows", axis=0, tiled=False)
    part = down_partial(
        device_count, down_row[:, 0], down_column, down_variant, gathered, hidden, down_weight, down_blocks
    )
    chunk = reduce_scatter(device_count, part)
    own_rows = set_count * tokens // device_count
    pieces = UNIT_ROWS // own_rows
    narrow = chunk.shape[-1]
    chunk = chunk.reshape(LANES, pieces, own_rows, narrow).transpose(2, 1, 0, 3)
    return chunk.reshape(own_rows, model_width)


def solution(mesh):
    in_specs = (
        P("groups", None),
        P(None, "rows"),
        P(None, "rows"),
        P("rows", None),
        P("rows", None, None),
        P("rows", None),
        P("rows"),
        P("rows"),
        P("rows"),
        P("rows", None, None),
        P("rows", None),
        P("rows"),
        P("rows"),
    )
    return jax.shard_map(
        on_device, mesh=mesh, in_specs=in_specs, out_specs=P(("groups", "rows"), None), check_vma=False
    )
```

```python
import functools

import jax
import jax.numpy as jnp
from jax import lax
from jax.experimental import pallas as pl
from jax.experimental.pallas import tpu as pltpu
from jax.sharding import PartitionSpec as P

VARIANTS = 23
UNIT_ROWS = 48
LANES = 4
VMEM_LIMIT = 56 * 1024 * 1024


def slot_ranks(targets):
    order = jnp.arange(targets.shape[0])
    earlier = (targets[:, None] == targets[None, :]) & (order[None, :] < order[:, None])
    return jnp.sum(earlier.astype(jnp.int32), axis=1)


def code_table(targets, ranks, codes, device_count, capacity):
    places = jnp.arange(device_count * capacity)
    hit = places[:, None] == (targets * capacity + ranks)[None, :]
    return jnp.sum(jnp.where(hit, codes[None, :], 0), axis=1).reshape(device_count, capacity)


VMEM = pl.BlockSpec(memory_space=pltpu.VMEM)
SMEM = pl.BlockSpec(memory_space=pltpu.SMEM)


def product_kernel(target_ref, slot_ref, row_ref, prompt_ref, block_ref, code_ref, out_ref):
    count = out_ref.shape[1] - 16
    out_ref[:, :count, :] = jnp.zeros((out_ref.shape[0], count, out_ref.shape[2]), jnp.bfloat16)
    out_ref[:, count:, :] = code_ref[...]
    batch = 8

    def body(step, _):
        parts = []
        for i in range(batch):
            j = step * batch + i
            columns = pl.ds(pl.multiple_of(row_ref[j] * 128, 128), 128)
            parts.append((j, jnp.dot(prompt_ref[:, columns], block_ref[j], preferred_element_type=jnp.float32)))
        for j, part in parts:
            rows = pl.ds(pl.multiple_of(slot_ref[j] * 16, 16), 16)
            out_ref[target_ref[j], rows, :] = part.astype(jnp.bfloat16)
        return 0

    lax.fori_loop(0, block_ref.shape[0] // batch, body, 0)


def exchange_kernel(device_count, with_base, *refs):
    if with_base:
        source, prompt_ref, gate_ref, up_ref, out_ref, gate_out, up_out, own_sem, send_sem, recv_sem = refs
    else:
        source, out_ref, own_sem, send_sem, recv_sem = refs
    me = lax.axis_index("rows")

    barrier = pltpu.get_barrier_semaphore()

    def greet(k, _):
        partner = lax.rem(me + k, device_count)
        pl.semaphore_signal(barrier, inc=1, device_id={"rows": partner}, device_id_type=pl.DeviceIdType.MESH)
        return 0

    lax.fori_loop(1, device_count, greet, 0)
    pl.semaphore_wait(barrier, device_count - 1)

    def transfer(k, place):
        partner = lax.rem(me + k, device_count)
        return pltpu.make_async_remote_copy(
            src_ref=source.at[partner],
            dst_ref=out_ref.at[place],
            send_sem=send_sem.at[k],
            recv_sem=recv_sem.at[k],
            device_id={"rows": partner},
            device_id_type=pl.DeviceIdType.MESH,
        )

    def launch(k, _):
        transfer(k, me).start()
        return 0

    lax.fori_loop(1, device_count, launch, 0)
    own = pltpu.make_async_copy(source.at[me], out_ref.at[me], own_sem)
    own.start()
    if with_base:
        tile = 1024
        gate_out[...] = jnp.zeros_like(gate_out)
        up_out[...] = jnp.zeros_like(up_out)

        def base(step, _):
            part = pl.ds(pl.multiple_of(step * tile, tile), tile)
            chosen = prompt_ref[:, part]
            gate_out[...] += jnp.dot(chosen, gate_ref[part, :], preferred_element_type=jnp.float32)
            up_out[...] += jnp.dot(chosen, up_ref[part, :], preferred_element_type=jnp.float32)
            return 0

        lax.fori_loop(0, prompt_ref.shape[1] // tile, base, 0)
    own.wait()

    def finish(k, _):
        copy = transfer(k, lax.rem(me - k + device_count, device_count))
        copy.wait_recv()
        copy.wait_send()
        return 0

    lax.fori_loop(1, device_count, finish, 0)


def exchange(device_count, collective_id, source, base=()):
    shapes = [jax.ShapeDtypeStruct(source.shape, source.dtype)]
    if base:
        tokens, width = base[0].shape[0], base[1].shape[1]
        shapes += [jax.ShapeDtypeStruct((tokens, width), jnp.float32)] * 2
    return pl.pallas_call(
        functools.partial(exchange_kernel, device_count, bool(base)),
        out_shape=shapes,
        in_specs=[VMEM] * (1 + len(base)),
        out_specs=[VMEM] * len(shapes),
        scratch_shapes=[
            pltpu.SemaphoreType.DMA,
            pltpu.SemaphoreType.DMA((device_count,)),
            pltpu.SemaphoreType.DMA((device_count,)),
        ],
        compiler_params=pltpu.CompilerParams(
            collective_id=collective_id, has_side_effects=True, vmem_limit_bytes=VMEM_LIMIT
        ),
    )(source, *base)


def hidden_kernel(capacity, code_ref, wish_ref, got_ref, gate_ref, up_ref, hidden_ref, reply_ref, sums):
    sets = hidden_ref.shape[0] // 16
    sums[...] = jnp.zeros_like(sums)

    def add(device, _):
        for slot in range(capacity):
            code = code_ref[device, slot]
            sums[code] += got_ref[device, slot * 16 : slot * 16 + 16, :].astype(jnp.float32)
        return 0

    lax.fori_loop(0, got_ref.shape[0], add, 0)

    def finish(number, _):
        live = (number > 0).astype(jnp.float32)
        gate = gate_ref[...] + live * sums[2 * number]
        up = up_ref[...] + live * sums[2 * number + 1]
        rows = pl.ds(pl.multiple_of(number * 16, 16), 16)
        hidden_ref[rows, :] = (jax.nn.silu(gate) * up).astype(jnp.bfloat16)
        return 0

    lax.fori_loop(0, sets, finish, 0)

    def answer(device, _):
        for slot in range(capacity):
            rows = pl.ds(pl.multiple_of(wish_ref[device, slot] * 16, 16), 16)
            reply_ref[device, slot * 16 : slot * 16 + 16, :] = hidden_ref[rows, :]
        return 0

    lax.fori_loop(0, reply_ref.shape[0], answer, 0)


def down_kernel(device_count, row_ref, slot_ref, column_ref, variant_ref, all_ref, own_ref, weight_ref, block_ref, out_ref, acc):
    total_rows, model_width = acc.shape
    tile = 1024

    def dense(step, _):
        columns = pl.ds(pl.multiple_of(step * tile, tile), tile)
        acc[:, columns] = jnp.dot(own_ref[...], weight_ref[:, columns], preferred_element_type=jnp.float32)
        return 0

    lax.fori_loop(0, model_width // tile, dense, 0)
    slots = block_ref.shape[0]
    batch = 8

    def correct(step, _):
        parts = []
        for i in range(batch):
            j = step * batch + i
            first = pl.multiple_of((variant_ref[j] + 1) * 16, 16)
            rows = all_ref[row_ref[j], pl.ds(pl.multiple_of(slot_ref[j] * 16, 16), 16), :]
            parts.append((j, first, jnp.dot(rows, block_ref[j], preferred_element_type=jnp.float32)))
        for j, first, part in parts:
            columns = pl.ds(pl.multiple_of(column_ref[j] * 128, 128), 128)
            acc[pl.ds(first, 16), columns] += part
        return 0

    lax.fori_loop(0, slots // batch, correct, 0)
    own_rows = total_rows // device_count
    pieces = UNIT_ROWS // own_rows
    width = model_width // pieces
    narrow = width // LANES
    owners = 24 // own_rows

    def pack(step, _):
        first = pl.multiple_of(step * 24, 24)
        for owner in range(owners):
            place = step * (owners // 2) + owner // 2
            for channel in range(LANES):
                low = channel * narrow
                parts = [
                    acc[pl.ds(first, 24), piece * width + low : piece * width + low + narrow][
                        owner * own_rows : (owner + 1) * own_rows
                    ]
                    for piece in range(pieces)
                ]
                out_ref[channel, owner % 2, place] = jnp.concatenate(parts, axis=0).astype(jnp.bfloat16)
        return 0

    lax.fori_loop(0, total_rows // 24, pack, 0)


def down_partial(device_count, row, slot, column, variant, gathered, own, weight, blocks):
    total_rows = own.shape[0]
    model_width = weight.shape[1]
    width = model_width * (total_rows // device_count) // UNIT_ROWS
    return pl.pallas_call(
        functools.partial(down_kernel, device_count),
        out_shape=jax.ShapeDtypeStruct(
            (LANES, 2, device_count // 2, UNIT_ROWS, width // LANES), jnp.bfloat16
        ),
        in_specs=[pl.BlockSpec(memory_space=pltpu.SMEM)] * 4 + [pl.BlockSpec(memory_space=pltpu.VMEM)] * 4,
        out_specs=pl.BlockSpec(memory_space=pltpu.VMEM),
        scratch_shapes=[pltpu.VMEM((total_rows, model_width), jnp.float32)],
        compiler_params=pltpu.CompilerParams(vmem_limit_bytes=VMEM_LIMIT),
    )(row, slot, column, variant, gathered, own, weight, blocks)


def bit_orders(device_count):
    if device_count == 32:
        return [[0, 1, 2, 3, 4], [0, 2, 1, 3, 4]]
    bits = device_count.bit_length() - 1
    middle = (bits + 1) // 2
    first, second = list(range(1, middle)), list(range(middle, bits))
    return [[0] + first + second, [0] + second + first]


def scatter_kernel(device_count, part_ref, out_ref, *scratch):
    stages = device_count.bit_length() - 1
    received = scratch[:stages]
    sending = (None,) + scratch[stages : 2 * stages - 1]
    kept = (None,) + scratch[2 * stages - 1 : 3 * stages - 2]
    send_sem, recv_sem = scratch[3 * stages - 2 :]
    me = lax.axis_index("rows")
    half = device_count // 2
    orders = [bit_orders(device_count)[c % 2] for c in range(LANES)]
    my_bits = [(me // (1 << b)) % 2 for b in range(stages)]
    partners = [me + (1 - 2 * my_bits[b]) * (1 << b) for b in range(stages)]

    barrier = pltpu.get_barrier_semaphore()
    for b in range(stages):
        pl.semaphore_signal(barrier, inc=1, device_id={"rows": partners[b]}, device_id_type=pl.DeviceIdType.MESH)
    pl.semaphore_wait(barrier, stages)

    def transfer(channel, stage):
        source = part_ref.at[channel, 1 - my_bits[0]] if stage == 0 else sending[stage].at[channel]
        return pltpu.make_async_remote_copy(
            src_ref=source,
            dst_ref=received[stage].at[channel],
            send_sem=send_sem.at[channel, stage],
            recv_sem=recv_sem.at[channel, stage],
            device_id={"rows": partners[orders[channel][stage]]},
            device_id_type=pl.DeviceIdType.MESH,
        )

    copies = {}
    for channel in range(LANES):
        copies[channel, 0] = transfer(channel, 0)
        copies[channel, 0].start()
    for stage in range(stages):
        count = half >> stage
        for channel in range(LANES):
            copies[channel, stage].wait_recv()

            def value(i):
                if stage == 0:
                    mine = part_ref[channel, my_bits[0], i].astype(jnp.float32)
                else:
                    mine = kept[stage][channel, i]
                return mine + received[stage][channel, i].astype(jnp.float32)

            if stage == stages - 1:
                out_ref[channel] = value(0).astype(jnp.bfloat16)
                continue
            bit = orders[channel][stage + 1]
            low = 1 << sum(1 for other in orders[channel][stage + 2 :] if other < bit)

            def pick(j, side):
                return (j // low) * (2 * low) + side * low + j % low

            def send_side(j, _):
                sending[stage + 1][channel, j] = value(pick(j, 1 - my_bits[bit])).astype(jnp.bfloat16)
                return 0

            def keep_side(j, _):
                kept[stage + 1][channel, j] = value(pick(j, my_bits[bit]))
                return 0

            lax.fori_loop(0, count // 2, send_side, 0)
            copies[channel, stage + 1] = transfer(channel, stage + 1)
            copies[channel, stage + 1].start()
            lax.fori_loop(0, count // 2, keep_side, 0)
    for copy in copies.values():
        copy.wait_send()


def reduce_scatter(device_count, part):
    narrow = part.shape[-1]
    stages = device_count.bit_length() - 1
    half = device_count // 2
    counts = [half >> s for s in range(stages)]
    scratch = [pltpu.VMEM((LANES, k, UNIT_ROWS, narrow), jnp.bfloat16) for k in counts]
    scratch += [pltpu.VMEM((LANES, k, UNIT_ROWS, narrow), jnp.bfloat16) for k in counts[1:]]
    scratch += [pltpu.VMEM((LANES, k, UNIT_ROWS, narrow), jnp.float32) for k in counts[1:]]
    scratch += [pltpu.SemaphoreType.DMA((LANES, stages))] * 2
    return pl.pallas_call(
        functools.partial(scatter_kernel, device_count),
        out_shape=jax.ShapeDtypeStruct((LANES, UNIT_ROWS, narrow), jnp.bfloat16),
        in_specs=[pl.BlockSpec(memory_space=pltpu.VMEM)],
        out_specs=pl.BlockSpec(memory_space=pltpu.VMEM),
        scratch_shapes=scratch,
        compiler_params=pltpu.CompilerParams(
            collective_id=0, has_side_effects=True, vmem_limit_bytes=VMEM_LIMIT
        ),
    )(part)


def on_device(
    prompt,
    gate_weight,
    up_weight,
    down_weight,
    proj_blocks,
    proj_column,
    proj_row,
    proj_variant,
    proj_kind,
    down_blocks,
    down_row,
    down_column,
    down_variant,
):
    device_count = lax.axis_size("rows")
    block_size = proj_blocks.shape[1]
    tokens, model_width = prompt.shape
    set_count = VARIANTS + 1
    slots = proj_blocks.shape[0]
    capacity = max(2, -(-slots // device_count))

    params = pltpu.CompilerParams(vmem_limit_bytes=VMEM_LIMIT)
    proj_target, down_target = proj_column[:, 0], down_row[:, 0]
    proj_slot, down_slot = slot_ranks(proj_target), slot_ranks(down_target)
    codes = jnp.concatenate(
        [
            code_table(proj_target, proj_slot, proj_variant * 2 + proj_kind + 2, device_count, capacity),
            code_table(down_target, down_slot, down_variant + 1, device_count, capacity),
            jnp.zeros((device_count, block_size - 2 * capacity), jnp.int32),
        ],
        axis=1,
    ).astype(jnp.bfloat16)
    codes = jnp.broadcast_to(codes[:, None, :], (device_count, 16, block_size))
    sent = pl.pallas_call(
        product_kernel,
        out_shape=jax.ShapeDtypeStruct((device_count, capacity * tokens + 16, block_size), jnp.bfloat16),
        in_specs=[SMEM] * 3 + [VMEM] * 3,
        out_specs=VMEM,
        compiler_params=params,
    )(proj_target, proj_slot, proj_row, prompt, proj_blocks, codes)
    got, gate_base, up_base = exchange(device_count, 1, sent, (prompt, gate_weight, up_weight))
    got_codes = got[:, capacity * tokens, : 2 * capacity].astype(jnp.int32)
    hidden, reply = pl.pallas_call(
        functools.partial(hidden_kernel, capacity),
        out_shape=[
            jax.ShapeDtypeStruct((set_count * tokens, block_size), jnp.bfloat16),
            jax.ShapeDtypeStruct((device_count, capacity * tokens, block_size), jnp.bfloat16),
        ],
        in_specs=[SMEM] * 2 + [VMEM] * 3,
        out_specs=[VMEM] * 2,
        scratch_shapes=[pltpu.VMEM((2 * set_count, tokens, block_size), jnp.float32)],
        compiler_params=params,
    )(got_codes[:, :capacity], got_codes[:, capacity:], got, gate_base, up_base)
    (gathered,) = exchange(device_count, 2, reply)
    part = down_partial(
        device_count, down_target, down_slot, down_column, down_variant, gathered, hidden, down_weight, down_blocks
    )
    chunk = reduce_scatter(device_count, part)
    own_rows = set_count * tokens // device_count
    pieces = UNIT_ROWS // own_rows
    narrow = chunk.shape[-1]
    chunk = chunk.reshape(LANES, pieces, own_rows, narrow).transpose(2, 1, 0, 3)
    return chunk.reshape(own_rows, model_width)


def solution(mesh):
    in_specs = (
        P("groups", None),
        P(None, "rows"),
        P(None, "rows"),
        P("rows", None),
        P("rows", None, None),
        P("rows", None),
        P("rows"),
        P("rows"),
        P("rows"),
        P("rows", None, None),
        P("rows", None),
        P("rows"),
        P("rows"),
    )
    return jax.shard_map(
        on_device, mesh=mesh, in_specs=in_specs, out_specs=P(("groups", "rows"), None), check_vma=False
    )
```

```python
import functools

import jax
import jax.numpy as jnp
from jax import lax
from jax.experimental import pallas as pl
from jax.experimental.pallas import tpu as pltpu
from jax.sharding import PartitionSpec as P

VARIANTS = 23
UNIT_ROWS = 48
VMEM_LIMIT = 56 * 1024 * 1024


def slot_ranks(targets):
    order = jnp.arange(targets.shape[0])
    earlier = (targets[:, None] == targets[None, :]) & (order[None, :] < order[:, None])
    return jnp.sum(earlier.astype(jnp.int32), axis=1)


def code_table(targets, ranks, codes, device_count, capacity):
    places = jnp.arange(device_count * capacity)
    hit = places[:, None] == (targets * capacity + ranks)[None, :]
    return jnp.sum(jnp.where(hit, codes[None, :], 0), axis=1).reshape(device_count, capacity)


VMEM = pl.BlockSpec(memory_space=pltpu.VMEM)
SMEM = pl.BlockSpec(memory_space=pltpu.SMEM)


def product_kernel(target_ref, slot_ref, row_ref, prompt_ref, block_ref, code_ref, out_ref):
    count = out_ref.shape[1] - 16
    out_ref[:, :count, :] = jnp.zeros((out_ref.shape[0], count, out_ref.shape[2]), jnp.bfloat16)
    out_ref[:, count:, :] = code_ref[...]
    batch = 8

    def body(step, _):
        parts = []
        for i in range(batch):
            j = step * batch + i
            columns = pl.ds(pl.multiple_of(row_ref[j] * 128, 128), 128)
            parts.append((j, jnp.dot(prompt_ref[:, columns], block_ref[j], preferred_element_type=jnp.float32)))
        for j, part in parts:
            rows = pl.ds(pl.multiple_of(slot_ref[j] * 16, 16), 16)
            out_ref[target_ref[j], rows, :] = part.astype(jnp.bfloat16)
        return 0

    lax.fori_loop(0, block_ref.shape[0] // batch, body, 0)


def exchange_kernel(device_count, with_base, *refs):
    if with_base:
        source, prompt_ref, gate_ref, up_ref, out_ref, gate_out, up_out, own_sem, send_sem, recv_sem = refs
    else:
        source, out_ref, own_sem, send_sem, recv_sem = refs
    me = lax.axis_index("rows")

    barrier = pltpu.get_barrier_semaphore()

    def greet(k, _):
        partner = lax.rem(me + k, device_count)
        pl.semaphore_signal(barrier, inc=1, device_id={"rows": partner}, device_id_type=pl.DeviceIdType.MESH)
        return 0

    lax.fori_loop(1, device_count, greet, 0)
    pl.semaphore_wait(barrier, device_count - 1)

    def transfer(k, place):
        partner = lax.rem(me + k, device_count)
        return pltpu.make_async_remote_copy(
            src_ref=source.at[partner],
            dst_ref=out_ref.at[place],
            send_sem=send_sem.at[k],
            recv_sem=recv_sem.at[k],
            device_id={"rows": partner},
            device_id_type=pl.DeviceIdType.MESH,
        )

    def launch(k, _):
        transfer(k, me).start()
        return 0

    lax.fori_loop(1, device_count, launch, 0)
    own = pltpu.make_async_copy(source.at[me], out_ref.at[me], own_sem)
    own.start()
    if with_base:
        tile = 1024
        gate_out[...] = jnp.zeros_like(gate_out)
        up_out[...] = jnp.zeros_like(up_out)

        def base(step, _):
            part = pl.ds(pl.multiple_of(step * tile, tile), tile)
            chosen = prompt_ref[:, part]
            gate_out[...] += jnp.dot(chosen, gate_ref[part, :], preferred_element_type=jnp.float32)
            up_out[...] += jnp.dot(chosen, up_ref[part, :], preferred_element_type=jnp.float32)
            return 0

        lax.fori_loop(0, prompt_ref.shape[1] // tile, base, 0)
    own.wait()

    def finish(k, _):
        copy = transfer(k, lax.rem(me - k + device_count, device_count))
        copy.wait_recv()
        copy.wait_send()
        return 0

    lax.fori_loop(1, device_count, finish, 0)


def exchange(device_count, collective_id, source, base=()):
    shapes = [jax.ShapeDtypeStruct(source.shape, source.dtype)]
    if base:
        tokens, width = base[0].shape[0], base[1].shape[1]
        shapes += [jax.ShapeDtypeStruct((tokens, width), jnp.float32)] * 2
    return pl.pallas_call(
        functools.partial(exchange_kernel, device_count, bool(base)),
        out_shape=shapes,
        in_specs=[VMEM] * (1 + len(base)),
        out_specs=[VMEM] * len(shapes),
        scratch_shapes=[
            pltpu.SemaphoreType.DMA,
            pltpu.SemaphoreType.DMA((device_count,)),
            pltpu.SemaphoreType.DMA((device_count,)),
        ],
        compiler_params=pltpu.CompilerParams(
            collective_id=collective_id, has_side_effects=True, vmem_limit_bytes=VMEM_LIMIT
        ),
    )(source, *base)


def hidden_kernel(capacity, code_ref, wish_ref, got_ref, gate_ref, up_ref, hidden_ref, reply_ref, sums):
    sets = hidden_ref.shape[0] // 16
    sums[...] = jnp.zeros_like(sums)

    def add(device, _):
        for slot in range(capacity):
            code = code_ref[device, slot]
            sums[code] += got_ref[device, slot * 16 : slot * 16 + 16, :].astype(jnp.float32)
        return 0

    lax.fori_loop(0, got_ref.shape[0], add, 0)

    def finish(number, _):
        live = (number > 0).astype(jnp.float32)
        gate = gate_ref[...] + live * sums[2 * number]
        up = up_ref[...] + live * sums[2 * number + 1]
        rows = pl.ds(pl.multiple_of(number * 16, 16), 16)
        hidden_ref[rows, :] = (jax.nn.silu(gate) * up).astype(jnp.bfloat16)
        return 0

    lax.fori_loop(0, sets, finish, 0)

    def answer(device, _):
        for slot in range(capacity):
            rows = pl.ds(pl.multiple_of(wish_ref[device, slot] * 16, 16), 16)
            reply_ref[device, slot * 16 : slot * 16 + 16, :] = hidden_ref[rows, :]
        return 0

    lax.fori_loop(0, reply_ref.shape[0], answer, 0)


def down_kernel(device_count, row_ref, slot_ref, column_ref, variant_ref, all_ref, own_ref, weight_ref, block_ref, out_ref, acc):
    total_rows, model_width = acc.shape
    tile = 1024

    def dense(step, _):
        columns = pl.ds(pl.multiple_of(step * tile, tile), tile)
        acc[:, columns] = jnp.dot(own_ref[...], weight_ref[:, columns], preferred_element_type=jnp.float32)
        return 0

    lax.fori_loop(0, model_width // tile, dense, 0)
    slots = block_ref.shape[0]
    batch = 8

    def correct(step, _):
        parts = []
        for i in range(batch):
            j = step * batch + i
            first = pl.multiple_of((variant_ref[j] + 1) * 16, 16)
            rows = all_ref[row_ref[j], pl.ds(pl.multiple_of(slot_ref[j] * 16, 16), 16), :]
            parts.append((j, first, jnp.dot(rows, block_ref[j], preferred_element_type=jnp.float32)))
        for j, first, part in parts:
            columns = pl.ds(pl.multiple_of(column_ref[j] * 128, 128), 128)
            acc[pl.ds(first, 16), columns] += part
        return 0

    lax.fori_loop(0, slots // batch, correct, 0)
    own_rows = total_rows // device_count
    pieces = UNIT_ROWS // own_rows
    width = model_width // pieces
    lanes = lanes_of(width)
    narrow = width // lanes
    owners = 24 // own_rows

    def pack(step, _):
        first = pl.multiple_of(step * 24, 24)
        for owner in range(owners):
            place = step * (owners // 2) + owner // 2
            for channel in range(lanes):
                low = channel * narrow
                parts = [
                    acc[pl.ds(first, 24), piece * width + low : piece * width + low + narrow][
                        owner * own_rows : (owner + 1) * own_rows
                    ]
                    for piece in range(pieces)
                ]
                out_ref[channel, owner % 2, place] = jnp.concatenate(parts, axis=0).astype(jnp.bfloat16)
        return 0

    lax.fori_loop(0, total_rows // 24, pack, 0)


def down_partial(device_count, row, slot, column, variant, gathered, own, weight, blocks):
    total_rows = own.shape[0]
    model_width = weight.shape[1]
    width = model_width * (total_rows // device_count) // UNIT_ROWS
    return pl.pallas_call(
        functools.partial(down_kernel, device_count),
        out_shape=jax.ShapeDtypeStruct(
            (lanes_of(width), 2, device_count // 2, UNIT_ROWS, width // lanes_of(width)), jnp.bfloat16
        ),
        in_specs=[pl.BlockSpec(memory_space=pltpu.SMEM)] * 4 + [pl.BlockSpec(memory_space=pltpu.VMEM)] * 4,
        out_specs=pl.BlockSpec(memory_space=pltpu.VMEM),
        scratch_shapes=[pltpu.VMEM((total_rows, model_width), jnp.float32)],
        compiler_params=pltpu.CompilerParams(vmem_limit_bytes=VMEM_LIMIT),
    )(row, slot, column, variant, gathered, own, weight, blocks)


def lanes_of(width):
    return min(8, width // 128)


def bit_orders(device_count):
    if device_count == 32:
        along_x, along_y = [0, 1, 2, 3, 4], [0, 2, 1, 3, 4]
        return [[0, 3, 4, 1, 2], along_x, along_y, along_x, along_y, [0, 3, 4, 2, 1], along_x, along_y]
    bits = device_count.bit_length() - 1
    middle = (bits + 1) // 2
    first, second = list(range(1, middle)), list(range(middle, bits))
    return [[0] + first + second, [0] + second + first] * 4


def scatter_kernel(device_count, part_ref, out_ref, *scratch):
    stages = device_count.bit_length() - 1
    received = scratch[:stages]
    sending = (None,) + scratch[stages : 2 * stages - 1]
    kept = (None,) + scratch[2 * stages - 1 : 3 * stages - 2]
    send_sem, recv_sem = scratch[3 * stages - 2 :]
    me = lax.axis_index("rows")
    half = device_count // 2
    lanes = part_ref.shape[0]
    orders = bit_orders(device_count)[:lanes]
    my_bits = [(me // (1 << b)) % 2 for b in range(stages)]
    partners = [me + (1 - 2 * my_bits[b]) * (1 << b) for b in range(stages)]

    barrier = pltpu.get_barrier_semaphore()
    for b in range(stages):
        pl.semaphore_signal(barrier, inc=1, device_id={"rows": partners[b]}, device_id_type=pl.DeviceIdType.MESH)
    pl.semaphore_wait(barrier, stages)

    def transfer(channel, stage):
        source = part_ref.at[channel, 1 - my_bits[0]] if stage == 0 else sending[stage].at[channel]
        return pltpu.make_async_remote_copy(
            src_ref=source,
            dst_ref=received[stage].at[channel],
            send_sem=send_sem.at[channel, stage],
            recv_sem=recv_sem.at[channel, stage],
            device_id={"rows": partners[orders[channel][stage]]},
            device_id_type=pl.DeviceIdType.MESH,
        )

    copies = {}
    for channel in range(lanes):
        copies[channel, 0] = transfer(channel, 0)
        copies[channel, 0].start()
    for stage in range(stages):
        count = half >> stage
        for channel in range(lanes):
            copies[channel, stage].wait_recv()

            def value(i):
                if stage == 0:
                    mine = part_ref[channel, my_bits[0], i].astype(jnp.float32)
                else:
                    mine = kept[stage][channel, i]
                return mine + received[stage][channel, i].astype(jnp.float32)

            if stage == stages - 1:
                final = value(0)
                own_rows, narrow = out_ref.shape[0], part_ref.shape[-1]
                for piece in range(UNIT_ROWS // own_rows):
                    low = (piece * lanes + channel) * narrow
                    out_ref[:, low : low + narrow] = final[piece * own_rows : (piece + 1) * own_rows]
                continue
            bit = orders[channel][stage + 1]
            low = 1 << sum(1 for other in orders[channel][stage + 2 :] if other < bit)

            def pick(j, side):
                return (j // low) * (2 * low) + side * low + j % low

            def send_side(j, _):
                sending[stage + 1][channel, j] = value(pick(j, 1 - my_bits[bit])).astype(jnp.bfloat16)
                return 0

            def keep_side(j, _):
                kept[stage + 1][channel, j] = value(pick(j, my_bits[bit]))
                return 0

            lax.fori_loop(0, count // 2, send_side, 0)
            copies[channel, stage + 1] = transfer(channel, stage + 1)
            copies[channel, stage + 1].start()
            lax.fori_loop(0, count // 2, keep_side, 0)
    for copy in copies.values():
        copy.wait_send()


def reduce_scatter(device_count, part, out_shape):
    lanes, narrow = part.shape[0], part.shape[-1]
    stages = device_count.bit_length() - 1
    half = device_count // 2
    counts = [half >> s for s in range(stages)]
    scratch = [pltpu.VMEM((lanes, k, UNIT_ROWS, narrow), jnp.bfloat16) for k in counts]
    scratch += [pltpu.VMEM((lanes, k, UNIT_ROWS, narrow), jnp.bfloat16) for k in counts[1:]]
    scratch += [pltpu.VMEM((lanes, k, UNIT_ROWS, narrow), jnp.float32) for k in counts[1:]]
    scratch += [pltpu.SemaphoreType.DMA((lanes, stages))] * 2
    return pl.pallas_call(
        functools.partial(scatter_kernel, device_count),
        out_shape=jax.ShapeDtypeStruct(out_shape, jnp.float32),
        in_specs=[pl.BlockSpec(memory_space=pltpu.VMEM)],
        out_specs=pl.BlockSpec(memory_space=pltpu.VMEM),
        scratch_shapes=scratch,
        compiler_params=pltpu.CompilerParams(
            collective_id=0, has_side_effects=True, vmem_limit_bytes=VMEM_LIMIT
        ),
    )(part)


def on_device(
    prompt,
    gate_weight,
    up_weight,
    down_weight,
    proj_blocks,
    proj_column,
    proj_row,
    proj_variant,
    proj_kind,
    down_blocks,
    down_row,
    down_column,
    down_variant,
):
    device_count = lax.axis_size("rows")
    block_size = proj_blocks.shape[1]
    tokens, model_width = prompt.shape
    set_count = VARIANTS + 1
    slots = proj_blocks.shape[0]
    capacity = max(2, -(-slots // device_count))

    params = pltpu.CompilerParams(vmem_limit_bytes=VMEM_LIMIT)
    proj_target, down_target = proj_column[:, 0], down_row[:, 0]
    proj_slot, down_slot = slot_ranks(proj_target), slot_ranks(down_target)
    codes = jnp.concatenate(
        [
            code_table(proj_target, proj_slot, proj_variant * 2 + proj_kind + 2, device_count, capacity),
            code_table(down_target, down_slot, down_variant + 1, device_count, capacity),
            jnp.zeros((device_count, block_size - 2 * capacity), jnp.int32),
        ],
        axis=1,
    ).astype(jnp.bfloat16)
    codes = jnp.broadcast_to(codes[:, None, :], (device_count, 16, block_size))
    sent = pl.pallas_call(
        product_kernel,
        out_shape=jax.ShapeDtypeStruct((device_count, capacity * tokens + 16, block_size), jnp.bfloat16),
        in_specs=[SMEM] * 3 + [VMEM] * 3,
        out_specs=VMEM,
        compiler_params=params,
    )(proj_target, proj_slot, proj_row, prompt, proj_blocks, codes)
    got, gate_base, up_base = exchange(device_count, 1, sent, (prompt, gate_weight, up_weight))
    got_codes = got[:, capacity * tokens, : 2 * capacity].astype(jnp.int32)
    hidden, reply = pl.pallas_call(
        functools.partial(hidden_kernel, capacity),
        out_shape=[
            jax.ShapeDtypeStruct((set_count * tokens, block_size), jnp.bfloat16),
            jax.ShapeDtypeStruct((device_count, capacity * tokens, block_size), jnp.bfloat16),
        ],
        in_specs=[SMEM] * 2 + [VMEM] * 3,
        out_specs=[VMEM] * 2,
        scratch_shapes=[pltpu.VMEM((2 * set_count, tokens, block_size), jnp.float32)],
        compiler_params=params,
    )(got_codes[:, :capacity], got_codes[:, capacity:], got, gate_base, up_base)
    (gathered,) = exchange(device_count, 2, reply)
    part = down_partial(
        device_count, down_target, down_slot, down_column, down_variant, gathered, hidden, down_weight, down_blocks
    )
    own_rows = set_count * tokens // device_count
    return reduce_scatter(device_count, part, (own_rows, model_width)).astype(jnp.bfloat16)


def solution(mesh):
    in_specs = (
        P("groups", None),
        P(None, "rows"),
        P(None, "rows"),
        P("rows", None),
        P("rows", None, None),
        P("rows", None),
        P("rows"),
        P("rows"),
        P("rows"),
        P("rows", None, None),
        P("rows", None),
        P("rows"),
        P("rows"),
    )
    return jax.shard_map(
        on_device, mesh=mesh, in_specs=in_specs, out_specs=P(("groups", "rows"), None), check_vma=False
    )
```

```python
import functools

import jax
import jax.numpy as jnp
from jax import lax
from jax.experimental import pallas as pl
from jax.experimental.pallas import tpu as pltpu
from jax.sharding import PartitionSpec as P

VARIANTS = 23
UNIT_ROWS = 48
VMEM_LIMIT = 30 * 1024 * 1024
SMALL_LIMIT = 10 * 1024 * 1024


def slot_ranks(targets):
    order = jnp.arange(targets.shape[0])
    earlier = (targets[:, None] == targets[None, :]) & (order[None, :] < order[:, None])
    return jnp.sum(earlier.astype(jnp.int32), axis=1)


def code_table(targets, ranks, codes, device_count, capacity):
    places = jnp.arange(device_count * capacity)
    hit = places[:, None] == (targets * capacity + ranks)[None, :]
    return jnp.sum(jnp.where(hit, codes[None, :], 0), axis=1).reshape(device_count, capacity)


VMEM = pl.BlockSpec(memory_space=pltpu.VMEM)
SMEM = pl.BlockSpec(memory_space=pltpu.SMEM)


def product_kernel(target_ref, slot_ref, row_ref, prompt_ref, block_ref, code_ref, out_ref):
    count = out_ref.shape[1] - 16
    out_ref[:, :count, :] = jnp.zeros((out_ref.shape[0], count, out_ref.shape[2]), jnp.bfloat16)
    out_ref[:, count:, :] = code_ref[...]
    batch = 8

    def body(step, _):
        parts = []
        for i in range(batch):
            j = step * batch + i
            columns = pl.ds(pl.multiple_of(row_ref[j] * 128, 128), 128)
            parts.append((j, jnp.dot(prompt_ref[:, columns], block_ref[j], preferred_element_type=jnp.float32)))
        for j, part in parts:
            rows = pl.ds(pl.multiple_of(slot_ref[j] * 16, 16), 16)
            out_ref[target_ref[j], rows, :] = part.astype(jnp.bfloat16)
        return 0

    lax.fori_loop(0, block_ref.shape[0] // batch, body, 0)


def exchange_kernel(device_count, with_base, *refs):
    if with_base:
        source, prompt_ref, gate_ref, up_ref, out_ref, gate_out, up_out, own_sem, send_sem, recv_sem = refs
    else:
        source, out_ref, own_sem, send_sem, recv_sem = refs
    me = lax.axis_index("rows")

    barrier = pltpu.get_barrier_semaphore()

    def greet(k, _):
        partner = lax.rem(me + k, device_count)
        pl.semaphore_signal(barrier, inc=1, device_id={"rows": partner}, device_id_type=pl.DeviceIdType.MESH)
        return 0

    lax.fori_loop(1, device_count, greet, 0)
    pl.semaphore_wait(barrier, device_count - 1)

    def transfer(k, place):
        partner = lax.rem(me + k, device_count)
        return pltpu.make_async_remote_copy(
            src_ref=source.at[partner],
            dst_ref=out_ref.at[place],
            send_sem=send_sem.at[k],
            recv_sem=recv_sem.at[k],
            device_id={"rows": partner},
            device_id_type=pl.DeviceIdType.MESH,
        )

    def launch(k, _):
        transfer(k, me).start()
        return 0

    lax.fori_loop(1, device_count, launch, 0)
    own = pltpu.make_async_copy(source.at[me], out_ref.at[me], own_sem)
    own.start()
    if with_base:
        tile = 1024
        gate_out[...] = jnp.zeros_like(gate_out)
        up_out[...] = jnp.zeros_like(up_out)

        def base(step, _):
            part = pl.ds(pl.multiple_of(step * tile, tile), tile)
            chosen = prompt_ref[:, part]
            gate_out[...] += jnp.dot(chosen, gate_ref[part, :], preferred_element_type=jnp.float32)
            up_out[...] += jnp.dot(chosen, up_ref[part, :], preferred_element_type=jnp.float32)
            return 0

        lax.fori_loop(0, prompt_ref.shape[1] // tile, base, 0)
    own.wait()

    def finish(k, _):
        copy = transfer(k, lax.rem(me - k + device_count, device_count))
        copy.wait_recv()
        copy.wait_send()
        return 0

    lax.fori_loop(1, device_count, finish, 0)


def exchange(device_count, collective_id, source, base=()):
    shapes = [jax.ShapeDtypeStruct(source.shape, source.dtype)]
    if base:
        tokens, width = base[0].shape[0], base[1].shape[1]
        shapes += [jax.ShapeDtypeStruct((tokens, width), jnp.float32)] * 2
    return pl.pallas_call(
        functools.partial(exchange_kernel, device_count, bool(base)),
        out_shape=shapes,
        in_specs=[VMEM] * (1 + len(base)),
        out_specs=[VMEM] * len(shapes),
        scratch_shapes=[
            pltpu.SemaphoreType.DMA,
            pltpu.SemaphoreType.DMA((device_count,)),
            pltpu.SemaphoreType.DMA((device_count,)),
        ],
        compiler_params=pltpu.CompilerParams(
            collective_id=collective_id, has_side_effects=True, vmem_limit_bytes=SMALL_LIMIT
        ),
    )(source, *base)


def hidden_kernel(capacity, code_ref, wish_ref, got_ref, gate_ref, up_ref, hidden_ref, reply_ref, sums):
    sets = hidden_ref.shape[0] // 16
    sums[...] = jnp.zeros_like(sums)

    def add(device, _):
        for slot in range(capacity):
            code = code_ref[device, slot]
            sums[code] += got_ref[device, slot * 16 : slot * 16 + 16, :].astype(jnp.float32)
        return 0

    lax.fori_loop(0, got_ref.shape[0], add, 0)

    def finish(number, _):
        live = (number > 0).astype(jnp.float32)
        gate = gate_ref[...] + live * sums[2 * number]
        up = up_ref[...] + live * sums[2 * number + 1]
        rows = pl.ds(pl.multiple_of(number * 16, 16), 16)
        hidden_ref[rows, :] = (jax.nn.silu(gate) * up).astype(jnp.bfloat16)
        return 0

    lax.fori_loop(0, sets, finish, 0)

    def answer(device, _):
        for slot in range(capacity):
            rows = pl.ds(pl.multiple_of(wish_ref[device, slot] * 16, 16), 16)
            reply_ref[device, slot * 16 : slot * 16 + 16, :] = hidden_ref[rows, :]
        return 0

    lax.fori_loop(0, reply_ref.shape[0], answer, 0)


def down_kernel(device_count, row_ref, slot_ref, column_ref, variant_ref, all_ref, own_ref, weight_ref, block_ref, out_ref, acc):
    total_rows, model_width = acc.shape
    tile = 1024

    def dense(step, _):
        columns = pl.ds(pl.multiple_of(step * tile, tile), tile)
        acc[:, columns] = jnp.dot(own_ref[...], weight_ref[:, columns], preferred_element_type=jnp.float32)
        return 0

    lax.fori_loop(0, model_width // tile, dense, 0)
    slots = block_ref.shape[0]
    batch = 8

    def correct(step, _):
        parts = []
        for i in range(batch):
            j = step * batch + i
            first = pl.multiple_of((variant_ref[j] + 1) * 16, 16)
            rows = all_ref[row_ref[j], pl.ds(pl.multiple_of(slot_ref[j] * 16, 16), 16), :]
            parts.append((j, first, jnp.dot(rows, block_ref[j], preferred_element_type=jnp.float32)))
        for j, first, part in parts:
            columns = pl.ds(pl.multiple_of(column_ref[j] * 128, 128), 128)
            acc[pl.ds(first, 16), columns] += part
        return 0

    lax.fori_loop(0, slots // batch, correct, 0)
    own_rows = total_rows // device_count
    pieces = UNIT_ROWS // own_rows
    width = model_width // pieces
    lanes = lanes_of(width)
    narrow = width // lanes
    owners = 24 // own_rows

    def pack(step, _):
        first = pl.multiple_of(step * 24, 24)
        for owner in range(owners):
            place = step * (owners // 2) + owner // 2
            for channel in range(lanes):
                low = channel * narrow
                parts = [
                    acc[pl.ds(first, 24), piece * width + low : piece * width + low + narrow][
                        owner * own_rows : (owner + 1) * own_rows
                    ]
                    for piece in range(pieces)
                ]
                out_ref[channel, owner % 2, place] = jnp.concatenate(parts, axis=0).astype(jnp.bfloat16)
        return 0

    lax.fori_loop(0, total_rows // 24, pack, 0)


def down_partial(device_count, row, slot, column, variant, gathered, own, weight, blocks):
    total_rows = own.shape[0]
    model_width = weight.shape[1]
    width = model_width * (total_rows // device_count) // UNIT_ROWS
    return pl.pallas_call(
        functools.partial(down_kernel, device_count),
        out_shape=jax.ShapeDtypeStruct(
            (lanes_of(width), 2, device_count // 2, UNIT_ROWS, width // lanes_of(width)), jnp.bfloat16
        ),
        in_specs=[pl.BlockSpec(memory_space=pltpu.SMEM)] * 4 + [pl.BlockSpec(memory_space=pltpu.VMEM)] * 4,
        out_specs=pl.BlockSpec(memory_space=pltpu.VMEM),
        scratch_shapes=[pltpu.VMEM((total_rows, model_width), jnp.float32)],
        compiler_params=pltpu.CompilerParams(vmem_limit_bytes=VMEM_LIMIT),
    )(row, slot, column, variant, gathered, own, weight, blocks)


def lanes_of(width):
    return min(8, width // 128)


def bit_orders(device_count):
    if device_count == 32:
        along_x, along_y = [0, 1, 2, 3, 4], [0, 2, 1, 3, 4]
        return [[0, 3, 4, 1, 2], along_x, along_y, along_x, along_y, [0, 3, 4, 2, 1], along_x, along_y]
    bits = device_count.bit_length() - 1
    middle = (bits + 1) // 2
    first, second = list(range(1, middle)), list(range(middle, bits))
    return [[0] + first + second, [0] + second + first] * 4


def scatter_kernel(device_count, part_ref, out_ref, *scratch):
    stages = device_count.bit_length() - 1
    received = scratch[:stages]
    sending = (None,) + scratch[stages : 2 * stages - 1]
    kept = (None,) + scratch[2 * stages - 1 : 3 * stages - 2]
    send_sem, recv_sem = scratch[3 * stages - 2 :]
    me = lax.axis_index("rows")
    half = device_count // 2
    lanes = part_ref.shape[0]
    orders = bit_orders(device_count)[:lanes]
    my_bits = [(me // (1 << b)) % 2 for b in range(stages)]
    partners = [me + (1 - 2 * my_bits[b]) * (1 << b) for b in range(stages)]

    barrier = pltpu.get_barrier_semaphore()
    for b in range(stages):
        pl.semaphore_signal(barrier, inc=1, device_id={"rows": partners[b]}, device_id_type=pl.DeviceIdType.MESH)
    pl.semaphore_wait(barrier, stages)

    def transfer(channel, stage):
        source = part_ref.at[channel, 1 - my_bits[0]] if stage == 0 else sending[stage].at[channel]
        return pltpu.make_async_remote_copy(
            src_ref=source,
            dst_ref=received[stage].at[channel],
            send_sem=send_sem.at[channel, stage],
            recv_sem=recv_sem.at[channel, stage],
            device_id={"rows": partners[orders[channel][stage]]},
            device_id_type=pl.DeviceIdType.MESH,
        )

    copies = {}
    for channel in range(lanes):
        copies[channel, 0] = transfer(channel, 0)
        copies[channel, 0].start()
    for stage in range(stages):
        count = half >> stage
        for channel in range(lanes):
            copies[channel, stage].wait_recv()

            def value(i):
                if stage == 0:
                    mine = part_ref[channel, my_bits[0], i].astype(jnp.float32)
                else:
                    mine = kept[stage][channel, i]
                return mine + received[stage][channel, i].astype(jnp.float32)

            if stage == stages - 1:
                final = value(0)
                own_rows, narrow = out_ref.shape[0], part_ref.shape[-1]
                for piece in range(UNIT_ROWS // own_rows):
                    low = (piece * lanes + channel) * narrow
                    out_ref[:, low : low + narrow] = final[piece * own_rows : (piece + 1) * own_rows]
                continue
            bit = orders[channel][stage + 1]
            low = 1 << sum(1 for other in orders[channel][stage + 2 :] if other < bit)

            def pick(j, side):
                return (j // low) * (2 * low) + side * low + j % low

            def send_side(j, _):
                sending[stage + 1][channel, j] = value(pick(j, 1 - my_bits[bit])).astype(jnp.bfloat16)
                return 0

            def keep_side(j, _):
                kept[stage + 1][channel, j] = value(pick(j, my_bits[bit]))
                return 0

            lax.fori_loop(0, count // 2, send_side, 0)
            copies[channel, stage + 1] = transfer(channel, stage + 1)
            copies[channel, stage + 1].start()
            lax.fori_loop(0, count // 2, keep_side, 0)
    for copy in copies.values():
        copy.wait_send()


def reduce_scatter(device_count, part, out_shape):
    lanes, narrow = part.shape[0], part.shape[-1]
    stages = device_count.bit_length() - 1
    half = device_count // 2
    counts = [half >> s for s in range(stages)]
    scratch = [pltpu.VMEM((lanes, k, UNIT_ROWS, narrow), jnp.bfloat16) for k in counts]
    scratch += [pltpu.VMEM((lanes, k, UNIT_ROWS, narrow), jnp.bfloat16) for k in counts[1:]]
    scratch += [pltpu.VMEM((lanes, k, UNIT_ROWS, narrow), jnp.float32) for k in counts[1:]]
    scratch += [pltpu.SemaphoreType.DMA((lanes, stages))] * 2
    return pl.pallas_call(
        functools.partial(scatter_kernel, device_count),
        out_shape=jax.ShapeDtypeStruct(out_shape, jnp.float32),
        in_specs=[pl.BlockSpec(memory_space=pltpu.VMEM)],
        out_specs=pl.BlockSpec(memory_space=pltpu.VMEM),
        scratch_shapes=scratch,
        compiler_params=pltpu.CompilerParams(
            collective_id=0, has_side_effects=True, vmem_limit_bytes=VMEM_LIMIT
        ),
    )(part)


def on_device(
    prompt,
    gate_weight,
    up_weight,
    down_weight,
    proj_blocks,
    proj_column,
    proj_row,
    proj_variant,
    proj_kind,
    down_blocks,
    down_row,
    down_column,
    down_variant,
):
    device_count = lax.axis_size("rows")
    block_size = proj_blocks.shape[1]
    tokens, model_width = prompt.shape
    set_count = VARIANTS + 1
    slots = proj_blocks.shape[0]
    capacity = max(2, -(-slots // device_count))

    params = pltpu.CompilerParams(vmem_limit_bytes=SMALL_LIMIT)
    proj_target, down_target = proj_column[:, 0], down_row[:, 0]
    proj_slot, down_slot = slot_ranks(proj_target), slot_ranks(down_target)
    codes = jnp.concatenate(
        [
            code_table(proj_target, proj_slot, proj_variant * 2 + proj_kind + 2, device_count, capacity),
            code_table(down_target, down_slot, down_variant + 1, device_count, capacity),
            jnp.zeros((device_count, block_size - 2 * capacity), jnp.int32),
        ],
        axis=1,
    ).astype(jnp.bfloat16)
    codes = jnp.broadcast_to(codes[:, None, :], (device_count, 16, block_size))
    sent = pl.pallas_call(
        product_kernel,
        out_shape=jax.ShapeDtypeStruct((device_count, capacity * tokens + 16, block_size), jnp.bfloat16),
        in_specs=[SMEM] * 3 + [VMEM] * 3,
        out_specs=VMEM,
        compiler_params=params,
    )(proj_target, proj_slot, proj_row, prompt, proj_blocks, codes)
    got, gate_base, up_base = exchange(device_count, 1, sent, (prompt, gate_weight, up_weight))
    got_codes = got[:, capacity * tokens, : 2 * capacity].astype(jnp.int32)
    hidden, reply = pl.pallas_call(
        functools.partial(hidden_kernel, capacity),
        out_shape=[
            jax.ShapeDtypeStruct((set_count * tokens, block_size), jnp.bfloat16),
            jax.ShapeDtypeStruct((device_count, capacity * tokens, block_size), jnp.bfloat16),
        ],
        in_specs=[SMEM] * 2 + [VMEM] * 3,
        out_specs=[VMEM] * 2,
        scratch_shapes=[pltpu.VMEM((2 * set_count, tokens, block_size), jnp.float32)],
        compiler_params=params,
    )(got_codes[:, :capacity], got_codes[:, capacity:], got, gate_base, up_base)
    (gathered,) = exchange(device_count, 2, reply)
    part = down_partial(
        device_count, down_target, down_slot, down_column, down_variant, gathered, hidden, down_weight, down_blocks
    )
    own_rows = set_count * tokens // device_count
    return reduce_scatter(device_count, part, (own_rows, model_width)).astype(jnp.bfloat16)


def solution(mesh):
    in_specs = (
        P("groups", None),
        P(None, "rows"),
        P(None, "rows"),
        P("rows", None),
        P("rows", None, None),
        P("rows", None),
        P("rows"),
        P("rows"),
        P("rows"),
        P("rows", None, None),
        P("rows", None),
        P("rows"),
        P("rows"),
    )
    return jax.shard_map(
        on_device, mesh=mesh, in_specs=in_specs, out_specs=P(("groups", "rows"), None), check_vma=False
    )
```

```python
import functools

import jax
import jax.numpy as jnp
from jax import lax
from jax.experimental import pallas as pl
from jax.experimental.pallas import tpu as pltpu
from jax.sharding import PartitionSpec as P

VARIANTS = 23
UNIT_ROWS = 48
VMEM_LIMIT = 30 * 1024 * 1024
SMALL_LIMIT = 10 * 1024 * 1024


def slot_ranks(targets):
    order = jnp.arange(targets.shape[0])
    earlier = (targets[:, None] == targets[None, :]) & (order[None, :] < order[:, None])
    return jnp.sum(earlier.astype(jnp.int32), axis=1)


def code_table(targets, ranks, codes, device_count, capacity):
    places = jnp.arange(device_count * capacity)
    hit = places[:, None] == (targets * capacity + ranks)[None, :]
    return jnp.sum(jnp.where(hit, codes[None, :], 0), axis=1).reshape(device_count, capacity)


VMEM = pl.BlockSpec(memory_space=pltpu.VMEM)
SMEM = pl.BlockSpec(memory_space=pltpu.SMEM)


def product_kernel(target_ref, slot_ref, row_ref, prompt_ref, block_ref, code_ref, out_ref):
    count = out_ref.shape[1] - 16
    out_ref[:, :count, :] = jnp.zeros((out_ref.shape[0], count, out_ref.shape[2]), jnp.bfloat16)
    out_ref[:, count:, :] = code_ref[...]
    batch = 8

    def body(step, _):
        parts = []
        for i in range(batch):
            j = step * batch + i
            columns = pl.ds(pl.multiple_of(row_ref[j] * 128, 128), 128)
            parts.append((j, jnp.dot(prompt_ref[:, columns], block_ref[j], preferred_element_type=jnp.float32)))
        for j, part in parts:
            rows = pl.ds(pl.multiple_of(slot_ref[j] * 16, 16), 16)
            out_ref[target_ref[j], rows, :] = part.astype(jnp.bfloat16)
        return 0

    lax.fori_loop(0, block_ref.shape[0] // batch, body, 0)


def exchange_kernel(device_count, with_base, *refs):
    if with_base:
        source, prompt_ref, gate_ref, up_ref, out_ref, gate_out, up_out, own_sem, send_sem, recv_sem = refs
    else:
        source, out_ref, own_sem, send_sem, recv_sem = refs
    me = lax.axis_index("rows")

    barrier = pltpu.get_barrier_semaphore()

    def greet(k, _):
        partner = lax.rem(me + k, device_count)
        pl.semaphore_signal(barrier, inc=1, device_id={"rows": partner}, device_id_type=pl.DeviceIdType.MESH)
        return 0

    lax.fori_loop(1, device_count, greet, 0)
    pl.semaphore_wait(barrier, device_count - 1)

    def transfer(k, place):
        partner = lax.rem(me + k, device_count)
        return pltpu.make_async_remote_copy(
            src_ref=source.at[partner],
            dst_ref=out_ref.at[place],
            send_sem=send_sem.at[k],
            recv_sem=recv_sem.at[k],
            device_id={"rows": partner},
            device_id_type=pl.DeviceIdType.MESH,
        )

    def launch(k, _):
        transfer(k, me).start()
        return 0

    lax.fori_loop(1, device_count, launch, 0)
    own = pltpu.make_async_copy(source.at[me], out_ref.at[me], own_sem)
    own.start()
    if with_base:
        tile = 1024
        gate_out[...] = jnp.zeros_like(gate_out)
        up_out[...] = jnp.zeros_like(up_out)

        def base(step, _):
            part = pl.ds(pl.multiple_of(step * tile, tile), tile)
            chosen = prompt_ref[:, part]
            gate_out[...] += jnp.dot(chosen, gate_ref[part, :], preferred_element_type=jnp.float32)
            up_out[...] += jnp.dot(chosen, up_ref[part, :], preferred_element_type=jnp.float32)
            return 0

        lax.fori_loop(0, prompt_ref.shape[1] // tile, base, 0)
    own.wait()

    def finish(k, _):
        copy = transfer(k, lax.rem(me - k + device_count, device_count))
        copy.wait_recv()
        copy.wait_send()
        return 0

    lax.fori_loop(1, device_count, finish, 0)


def exchange(device_count, collective_id, source, base=()):
    shapes = [jax.ShapeDtypeStruct(source.shape, source.dtype)]
    if base:
        tokens, width = base[0].shape[0], base[1].shape[1]
        shapes += [jax.ShapeDtypeStruct((tokens, width), jnp.float32)] * 2
    return pl.pallas_call(
        functools.partial(exchange_kernel, device_count, bool(base)),
        out_shape=shapes,
        in_specs=[VMEM] * (1 + len(base)),
        out_specs=[VMEM] * len(shapes),
        scratch_shapes=[
            pltpu.SemaphoreType.DMA,
            pltpu.SemaphoreType.DMA((device_count,)),
            pltpu.SemaphoreType.DMA((device_count,)),
        ],
        compiler_params=pltpu.CompilerParams(
            collective_id=collective_id, has_side_effects=True, vmem_limit_bytes=SMALL_LIMIT
        ),
    )(source, *base)


def hidden_kernel(capacity, code_ref, wish_ref, got_ref, gate_ref, up_ref, hidden_ref, reply_ref, sums):
    sets = hidden_ref.shape[0] // 16
    sums[...] = jnp.zeros_like(sums)

    def add(device, _):
        for slot in range(capacity):
            code = code_ref[device, slot]
            sums[code] += got_ref[device, slot * 16 : slot * 16 + 16, :].astype(jnp.float32)
        return 0

    lax.fori_loop(0, got_ref.shape[0], add, 0)

    def finish(number, _):
        live = (number > 0).astype(jnp.float32)
        gate = gate_ref[...] + live * sums[2 * number]
        up = up_ref[...] + live * sums[2 * number + 1]
        rows = pl.ds(pl.multiple_of(number * 16, 16), 16)
        hidden_ref[rows, :] = (jax.nn.silu(gate) * up).astype(jnp.bfloat16)
        return 0

    lax.fori_loop(0, sets, finish, 0)

    def answer(device, _):
        for slot in range(capacity):
            rows = pl.ds(pl.multiple_of(wish_ref[device, slot] * 16, 16), 16)
            reply_ref[device, slot * 16 : slot * 16 + 16, :] = hidden_ref[rows, :]
        return 0

    lax.fori_loop(0, reply_ref.shape[0], answer, 0)


def down_kernel(device_count, row_ref, slot_ref, column_ref, variant_ref, all_ref, own_ref, weight_ref, block_ref, out_ref, acc):
    total_rows, model_width = acc.shape
    tile = 1024

    def dense(step, _):
        columns = pl.ds(pl.multiple_of(step * tile, tile), tile)
        acc[:, columns] = jnp.dot(own_ref[...], weight_ref[:, columns], preferred_element_type=jnp.float32)
        return 0

    lax.fori_loop(0, model_width // tile, dense, 0)
    slots = block_ref.shape[0]
    batch = 8

    def correct(step, _):
        parts = []
        for i in range(batch):
            j = step * batch + i
            first = pl.multiple_of((variant_ref[j] + 1) * 16, 16)
            rows = all_ref[row_ref[j], pl.ds(pl.multiple_of(slot_ref[j] * 16, 16), 16), :]
            parts.append((j, first, jnp.dot(rows, block_ref[j], preferred_element_type=jnp.float32)))
        for j, first, part in parts:
            columns = pl.ds(pl.multiple_of(column_ref[j] * 128, 128), 128)
            acc[pl.ds(first, 16), columns] += part
        return 0

    lax.fori_loop(0, slots // batch, correct, 0)
    own_rows = total_rows // device_count
    pieces = UNIT_ROWS // own_rows
    width = model_width // pieces
    lanes = lanes_of(width)
    narrow = width // lanes
    owners = 24 // own_rows

    def pack(step, _):
        first = pl.multiple_of(step * 24, 24)
        for owner in range(owners):
            place = step * (owners // 2) + owner // 2
            for channel in range(lanes):
                low = channel * narrow
                parts = [
                    acc[pl.ds(first, 24), piece * width + low : piece * width + low + narrow][
                        owner * own_rows : (owner + 1) * own_rows
                    ]
                    for piece in range(pieces)
                ]
                out_ref[channel, owner % 2, place] = jnp.concatenate(parts, axis=0).astype(jnp.bfloat16)
        return 0

    lax.fori_loop(0, total_rows // 24, pack, 0)


def down_partial(device_count, row, slot, column, variant, gathered, own, weight, blocks):
    total_rows = own.shape[0]
    model_width = weight.shape[1]
    width = model_width * (total_rows // device_count) // UNIT_ROWS
    return pl.pallas_call(
        functools.partial(down_kernel, device_count),
        out_shape=jax.ShapeDtypeStruct(
            (lanes_of(width), 2, device_count // 2, UNIT_ROWS, width // lanes_of(width)), jnp.bfloat16
        ),
        in_specs=[pl.BlockSpec(memory_space=pltpu.SMEM)] * 4 + [pl.BlockSpec(memory_space=pltpu.VMEM)] * 4,
        out_specs=pl.BlockSpec(memory_space=pltpu.VMEM),
        scratch_shapes=[pltpu.VMEM((total_rows, model_width), jnp.float32)],
        compiler_params=pltpu.CompilerParams(vmem_limit_bytes=VMEM_LIMIT),
    )(row, slot, column, variant, gathered, own, weight, blocks)


def lanes_of(width):
    return min(8, width // 128)


def bit_orders(device_count):
    if device_count == 32:
        along_x, along_y = [0, 1, 2, 3, 4], [0, 2, 1, 3, 4]
        return [[0, 3, 4, 1, 2], along_x, along_y, along_x, along_y, [0, 3, 4, 2, 1], along_x, along_y]
    bits = device_count.bit_length() - 1
    middle = (bits + 1) // 2
    first, second = list(range(1, middle)), list(range(middle, bits))
    return [[0] + first + second, [0] + second + first] * 4


def scatter_kernel(device_count, part_ref, out_ref, *scratch):
    stages = device_count.bit_length() - 1
    received = scratch[:stages]
    sending = (None,) + scratch[stages : 2 * stages - 1]
    kept = (None,) + scratch[2 * stages - 1 : 3 * stages - 2]
    send_sem, recv_sem = scratch[3 * stages - 2 :]
    me = lax.axis_index("rows")
    half = device_count // 2
    lanes = part_ref.shape[0]
    orders = bit_orders(device_count)[:lanes]
    my_bits = [(me // (1 << b)) % 2 for b in range(stages)]
    partners = [me + (1 - 2 * my_bits[b]) * (1 << b) for b in range(stages)]

    barrier = pltpu.get_barrier_semaphore()
    for b in range(stages):
        pl.semaphore_signal(barrier, inc=1, device_id={"rows": partners[b]}, device_id_type=pl.DeviceIdType.MESH)
    pl.semaphore_wait(barrier, stages)

    def transfer(channel, stage):
        source = part_ref.at[channel, 1 - my_bits[0]] if stage == 0 else sending[stage].at[channel]
        return pltpu.make_async_remote_copy(
            src_ref=source,
            dst_ref=received[stage].at[channel],
            send_sem=send_sem.at[channel, stage],
            recv_sem=recv_sem.at[channel, stage],
            device_id={"rows": partners[orders[channel][stage]]},
            device_id_type=pl.DeviceIdType.MESH,
        )

    copies = {}
    for channel in range(lanes):
        copies[channel, 0] = transfer(channel, 0)
        copies[channel, 0].start()
    steps = [(stage, channel) for stage in range(stages) for channel in range(lanes)]
    steps.sort(key=lambda step: (step[0] > 0, 4 * step[0] + step[1], step[0]))
    for stage, channel in steps:
        count = half >> stage
        copies[channel, stage].wait_recv()

        def value(i):
            if stage == 0:
                mine = part_ref[channel, my_bits[0], i].astype(jnp.float32)
            else:
                mine = kept[stage][channel, i]
            return mine + received[stage][channel, i].astype(jnp.float32)

        if stage == stages - 1:
            final = value(0)
            own_rows, narrow = out_ref.shape[0], part_ref.shape[-1]
            for piece in range(UNIT_ROWS // own_rows):
                low = (piece * lanes + channel) * narrow
                out_ref[:, low : low + narrow] = final[piece * own_rows : (piece + 1) * own_rows]
            continue
        bit = orders[channel][stage + 1]
        low = 1 << sum(1 for other in orders[channel][stage + 2 :] if other < bit)

        def pick(j, side):
            return (j // low) * (2 * low) + side * low + j % low

        def send_side(j, _):
            sending[stage + 1][channel, j] = value(pick(j, 1 - my_bits[bit])).astype(jnp.bfloat16)
            return 0

        def keep_side(j, _):
            kept[stage + 1][channel, j] = value(pick(j, my_bits[bit]))
            return 0

        lax.fori_loop(0, count // 2, send_side, 0)
        copies[channel, stage + 1] = transfer(channel, stage + 1)
        copies[channel, stage + 1].start()
        lax.fori_loop(0, count // 2, keep_side, 0)
    for copy in copies.values():
        copy.wait_send()


def reduce_scatter(device_count, part, out_shape):
    lanes, narrow = part.shape[0], part.shape[-1]
    stages = device_count.bit_length() - 1
    half = device_count // 2
    counts = [half >> s for s in range(stages)]
    scratch = [pltpu.VMEM((lanes, k, UNIT_ROWS, narrow), jnp.bfloat16) for k in counts]
    scratch += [pltpu.VMEM((lanes, k, UNIT_ROWS, narrow), jnp.bfloat16) for k in counts[1:]]
    scratch += [pltpu.VMEM((lanes, k, UNIT_ROWS, narrow), jnp.float32) for k in counts[1:]]
    scratch += [pltpu.SemaphoreType.DMA((lanes, stages))] * 2
    return pl.pallas_call(
        functools.partial(scatter_kernel, device_count),
        out_shape=jax.ShapeDtypeStruct(out_shape, jnp.float32),
        in_specs=[pl.BlockSpec(memory_space=pltpu.VMEM)],
        out_specs=pl.BlockSpec(memory_space=pltpu.VMEM),
        scratch_shapes=scratch,
        compiler_params=pltpu.CompilerParams(
            collective_id=0, has_side_effects=True, vmem_limit_bytes=VMEM_LIMIT
        ),
    )(part)


def on_device(
    prompt,
    gate_weight,
    up_weight,
    down_weight,
    proj_blocks,
    proj_column,
    proj_row,
    proj_variant,
    proj_kind,
    down_blocks,
    down_row,
    down_column,
    down_variant,
):
    device_count = lax.axis_size("rows")
    block_size = proj_blocks.shape[1]
    tokens, model_width = prompt.shape
    set_count = VARIANTS + 1
    slots = proj_blocks.shape[0]
    capacity = max(2, -(-slots // device_count))

    params = pltpu.CompilerParams(vmem_limit_bytes=SMALL_LIMIT)
    proj_target, down_target = proj_column[:, 0], down_row[:, 0]
    proj_slot, down_slot = slot_ranks(proj_target), slot_ranks(down_target)
    codes = jnp.concatenate(
        [
            code_table(proj_target, proj_slot, proj_variant * 2 + proj_kind + 2, device_count, capacity),
            code_table(down_target, down_slot, down_variant + 1, device_count, capacity),
            jnp.zeros((device_count, block_size - 2 * capacity), jnp.int32),
        ],
        axis=1,
    ).astype(jnp.bfloat16)
    codes = jnp.broadcast_to(codes[:, None, :], (device_count, 16, block_size))
    sent = pl.pallas_call(
        product_kernel,
        out_shape=jax.ShapeDtypeStruct((device_count, capacity * tokens + 16, block_size), jnp.bfloat16),
        in_specs=[SMEM] * 3 + [VMEM] * 3,
        out_specs=VMEM,
        compiler_params=params,
    )(proj_target, proj_slot, proj_row, prompt, proj_blocks, codes)
    got, gate_base, up_base = exchange(device_count, 1, sent, (prompt, gate_weight, up_weight))
    got_codes = got[:, capacity * tokens, : 2 * capacity].astype(jnp.int32)
    hidden, reply = pl.pallas_call(
        functools.partial(hidden_kernel, capacity),
        out_shape=[
            jax.ShapeDtypeStruct((set_count * tokens, block_size), jnp.bfloat16),
            jax.ShapeDtypeStruct((device_count, capacity * tokens, block_size), jnp.bfloat16),
        ],
        in_specs=[SMEM] * 2 + [VMEM] * 3,
        out_specs=[VMEM] * 2,
        scratch_shapes=[pltpu.VMEM((2 * set_count, tokens, block_size), jnp.float32)],
        compiler_params=params,
    )(got_codes[:, :capacity], got_codes[:, capacity:], got, gate_base, up_base)
    (gathered,) = exchange(device_count, 2, reply)
    part = down_partial(
        device_count, down_target, down_slot, down_column, down_variant, gathered, hidden, down_weight, down_blocks
    )
    own_rows = set_count * tokens // device_count
    return reduce_scatter(device_count, part, (own_rows, model_width)).astype(jnp.bfloat16)


def solution(mesh):
    in_specs = (
        P("groups", None),
        P(None, "rows"),
        P(None, "rows"),
        P("rows", None),
        P("rows", None, None),
        P("rows", None),
        P("rows"),
        P("rows"),
        P("rows"),
        P("rows", None, None),
        P("rows", None),
        P("rows"),
        P("rows"),
    )
    return jax.shard_map(
        on_device, mesh=mesh, in_specs=in_specs, out_specs=P(("groups", "rows"), None), check_vma=False
    )
```
